128 devices in a mesh: tm: 16 (over z_lo, x, core), rows: 8 (over y, z_hi).
Axes of the slice: x: 4, y: 4, z: 4 (z_hi: 2, z_lo: 2; z = z_hi * 2 + z_lo), core: 2. Of those that a mesh axis runs over, the one named last changes fastest.
Arguments:
- latents: bfloat16 [16, 96, 160, 384], P('tm', 'rows'), may hold values from -6 to 6
- norm_gain_one: float32 [384], replicated, may hold values from 0.5 to 2
- conv_weight_one: bfloat16 [10368, 384], replicated, may hold values from -0.0625 to 0.0625
- conv_bias_one: float32 [384], replicated, may hold values from -3 to 3
- norm_gain_two: float32 [384], replicated, may hold values from 0.5 to 2
- conv_weight_two: bfloat16 [10368, 384], replicated, may hold values from -0.0625 to 0.0625
- conv_bias_two: float32 [384], replicated, may hold values from -3 to 3
Outputs:
- block_out: bfloat16 [16, 96, 160, 384], P('tm', 'rows')
The draws below stay inside these ranges and needn't reach their ends.
All inputs are finite; a program needn't handle non-finite values.
Results may differ from the reference program's by a relative error of at most 0.0041.
Values may be sent and summed in bfloat16 or wider, within the bound.
A program may use at most 128 MiB of HBM per device.

```python
import math
import jax
import jax.numpy as jnp
from jax import lax

C = 384
COLS = 160
FRAMES = 16
ROWS = 96


def shard_levels(stream_key, extent, split, least, high):
    level, own = 1.0, jax.random.fold_in(stream_key, 6)
    for axis_at, blocks in split:
        steps = jnp.exp(jax.random.uniform(jax.random.fold_in(own, axis_at), (blocks,), jnp.float32, least / len(split), high / len(split)))
        level = level * jnp.repeat(steps, extent[axis_at] // blocks).reshape([-1 if axis == axis_at else 1 for axis in range(len(extent))])
    return level


def gaussian(key, dims, scale, limit, shards=(), kind=jnp.bfloat16):
    array = scale * jax.random.normal(key, dims, jnp.float32)
    if shards:
        array = array * shard_levels(key, dims, shards, -0.22, 0.18)
    return jnp.clip(array, -limit, limit).astype(kind)


def setup_inputs(seed: int = 0) -> dict:
    keys = jax.random.split(jax.random.key(seed), 8)
    return {
        "latents": gaussian(keys[0], (FRAMES, ROWS, COLS, C), 1.0, 6.0, ((0, 16), (1, 8))),
        "norm_gain_one": jnp.clip(jnp.exp(jax.random.uniform(keys[1], (C,), jnp.float32, math.log(0.5), math.log(2.0))), 0.5, 2.0),
        "conv_weight_one": gaussian(keys[2], (27 * C, C), (27 * C) ** -0.5, 0.0625),
        "conv_bias_one": gaussian(keys[3], (C,), 0.5, 3.0, (), jnp.float32),
        "norm_gain_two": jnp.clip(jnp.exp(jax.random.uniform(keys[4], (C,), jnp.float32, math.log(0.5), math.log(2.0))), 0.5, 2.0),
        "conv_weight_two": gaussian(keys[5], (27 * C, C), (27 * C) ** -0.5, 0.0625),
        "conv_bias_two": gaussian(keys[6], (C,), 0.5, 3.0, (), jnp.float32),
    }


def norm_act(values, gain):
    wide = values.astype(jnp.float32)
    scaled = wide * lax.rsqrt(lax.optimization_barrier(jnp.mean(wide * wide, axis=-1, keepdims=True)) + 1e-06) * gain
    return jax.nn.silu(scaled)

def convolve_frame(extended, weight):
    height = extended.shape[1] - 2
    width = extended.shape[2] - 2
    channels = extended.shape[3]
    taps = weight.reshape(3, 3, 3 * channels, channels)
    total = jnp.zeros((height * width, channels), jnp.float32)
    for frame_tap in range(3):
        for row_tap in range(3):
            window = extended[frame_tap, row_tap:row_tap + height]
            joined = jnp.concatenate([window[:, col_tap:col_tap + width] for col_tap in range(3)], axis=-1)
            total = total + jnp.dot(joined.reshape(height * width, 3 * channels), taps[frame_tap, row_tap], preferred_element_type=jnp.float32)
    return total.reshape(height, width, channels)

def convolve(field, weight, bias):
    padded = jnp.pad(field, ((2, 0), (1, 1), (1, 1), (0, 0)))

    def one_frame(frame):
        extended = lax.dynamic_slice_in_dim(padded, frame, 3, 0)
        return convolve_frame(extended, weight)
    frames_out = lax.map(one_frame, jnp.arange(field.shape[0], dtype=jnp.int32))
    return frames_out + bias

def reference(latents, norm_gain_one, conv_weight_one, conv_bias_one, norm_gain_two, conv_weight_two, conv_bias_two):
    first = norm_act(latents, norm_gain_one).astype(jnp.bfloat16)
    middle = convolve(first, conv_weight_one, conv_bias_one)
    second = norm_act(middle, norm_gain_two).astype(jnp.bfloat16)
    result = convolve(second, conv_weight_two, conv_bias_two) + latents.astype(jnp.float32)
    return result.astype(jnp.bfloat16)
```

```python
import functools

import jax
import jax.numpy as jnp
from jax import lax
from jax.experimental import pallas as pl
from jax.experimental.pallas import tpu as pltpu
from jax.sharding import PartitionSpec as P

MESH = pl.DeviceIdType.MESH
F32, BF16 = jnp.float32, jnp.bfloat16

C = 384
LANES = C // 128
H = 12
COLS = 160
N = 16
W = COLS // N
WH = W + 2
QI, RI = 3, 4
QO, RO = 4, 3
PI = RI * WH
PO = 32
PAIRS = 5


def norm_act(v, gain):
    scale = lax.rsqrt(jnp.mean(v * v, axis=-1, keepdims=True) + 1e-06)
    u = v * scale * gain
    return u / (1.0 + jnp.exp(-u))


def later(v, frames):
    at = lax.broadcasted_iota(jnp.int32, v.shape, v.ndim - 2)
    return jnp.where(at < frames, 0.0, pltpu.roll(v, frames, v.ndim - 2))


def peer(me, k):
    z, x, c = me // 8, (me // 2) % 4, me % 2
    dz, dx, dc = k // 8, (k // 2) % 4, k % 2
    return ((z + dz) % 2) * 8 + ((x + dx) % 4) * 2 + (c + dc) % 2


def source(me, k):
    z, x, c = me // 8, (me // 2) % 4, me % 2
    dz, dx, dc = k // 8, (k // 2) % 4, k % 2
    return ((z + dz) % 2) * 8 + ((x + 4 - dx) % 4) * 2 + (c + dc) % 2


ORDER = (12, 13, 4, 5, 10, 11, 14, 15, 2, 3, 6, 7, 8, 9, 1)


def kernel(
    lat, g1, w1, b1, g2, w2, b2,
    out,
    wc1, wc2, field, second, recv, send, nrm, pk, tr, prod, otr, ostage,
    w_sem, in_send, in_recv, f_send, f_recv, c_send, c_recv, r_send, r_recv, d_send, d_recv,
    out_send, out_recv, own_sem,
):
    me = lax.axis_index("tm")
    row = lax.axis_index("rows")
    left, right = (me + N - 1) % N, (me + 1) % N
    up, down = (row + 7) % 8, (row + 1) % 8

    def weight(i, w, wc, a):
        return pltpu.make_async_copy(
            w.at[pl.ds(a * 9 * C, 9 * C)], wc.at[:, pl.ds((2 - a) * C, C)], w_sem.at[i, a]
        )

    for i, (w, wc) in enumerate(((w1, wc1), (w2, wc2))):
        for a in range(3):
            weight(i, w, wc, a).start()

    barrier = pltpu.get_barrier_semaphore()
    for k in range(1, N):
        pl.semaphore_signal(barrier, inc=1, device_id=(peer(me, k), row), device_id_type=MESH)
    for dev in ((me, up), (me, down), (left, up), (left, down), (right, up), (right, down)):
        pl.semaphore_signal(barrier, inc=1, device_id=dev, device_id_type=MESH)

    nrm[:, 0:8] = jnp.zeros((H, 8, C), F32)
    nrm[:, 8 + COLS : 16 + COLS] = jnp.zeros((H, 8, C), F32)
    otr[...] = jnp.zeros_like(otr)

    def in_copy(q, k):
        return pltpu.make_async_remote_copy(
            src_ref=send.at[q, peer(me, k)],
            dst_ref=recv.at[q, me],
            send_sem=in_send.at[q, k],
            recv_sem=in_recv.at[q, k],
            device_id=(peer(me, k), row),
            device_id_type=MESH,
        )

    def in_arrival(q, k):
        return pltpu.make_async_remote_copy(
            src_ref=send.at[q, peer(me, k)],
            dst_ref=recv.at[q, source(me, k)],
            send_sem=in_send.at[q, k],
            recv_sem=in_recv.at[q, k],
            device_id=(peer(me, k), row),
            device_id_type=MESH,
        )

    gain1 = g1[...].reshape(1, C)
    for q in range(QI):

        def norm_row(r, _):
            nrm[r, 8 : 8 + COLS] = norm_act(lat[r].astype(F32), gain1)
            return 0

        lax.fori_loop(q * RI, (q + 1) * RI, norm_row, 0)
        for j in range(N):
            for r in range(RI):
                pk[j % 4, r * WH : (r + 1) * WH] = nrm[q * RI + r, j * W + 7 : j * W + 7 + WH]
            send[q, j] = pk[j % 4].astype(BF16)
        recv[q, me] = send[q, me]
        if q == 0:
            pl.semaphore_wait(barrier, N - 1 + 6)
        for k in ORDER:
            in_copy(q, k).start()

    def row_halo(i, ref, at, to, dev, s_sem, r_sem):
        return pltpu.make_async_remote_copy(
            src_ref=ref.at[at], dst_ref=ref.at[to], send_sem=s_sem.at[i], recv_sem=r_sem.at[i],
            device_id=dev, device_id_type=MESH,
        )

    field_up = row_halo(0, field, 1, H + 1, (me, up), f_send, f_recv)
    field_down = row_halo(1, field, H, 0, (me, down), f_send, f_recv)

    def arrive(q):
        for k in ORDER:
            in_arrival(q, k).wait_recv()

        def widen(f, _):
            v = recv[q, f].astype(F32)
            for lane in range(LANES):
                tr[lane, pl.ds(f * PI, PI)] = v[:, lane * 128 : (lane + 1) * 128]
            return 0

        lax.fori_loop(0, N, widen, 0)

        def turn(r, _):
            for c in range(WH):
                v = [tr[lane, pl.ds(r * WH + c, N, stride=PI)] for lane in range(LANES)]
                field[1 + q * RI + r, c] = jnp.concatenate(v, axis=-1).astype(BF16)
            return 0

        lax.fori_loop(0, RI, turn, 0)

    def multiply(src, wc, r0, rows):
        taps = [
            src[pl.ds(r0 + b, rows), e : e + W].reshape(rows * W * N, C)
            for b in range(3) for e in range(3)
        ]
        prod[0 : rows * W * N] = jnp.dot(
            jnp.concatenate(taps, axis=-1), wc[...], preferred_element_type=F32
        )

    def collect(px, count):
        v = prod[pl.ds(px * N, count * N)].reshape(count, N, 3 * C)
        return v[:, :, :C] + later(v[:, :, C : 2 * C], 1) + later(v[:, :, 2 * C :], 2)

    def first_rows(r0, rows):
        multiply(field, wc1, r0, rows)
        for r in range(rows):

            def finish(c, _):
                v = collect(r * W + c * 2, 2) + b1[...].reshape(1, C)
                second[r0 + r + 1, pl.ds(1 + c * 2, 2)] = norm_act(v, g2[...].reshape(1, C)).astype(BF16)
                return 0

            lax.fori_loop(0, W // 2, finish, 0)

    def side(i, r0, rows, which):
        src, dst, dev = ((1, W + 1, left), (W, 0, right))[which]
        return pltpu.make_async_remote_copy(
            src_ref=second.at[pl.ds(r0 + 1, rows), pl.ds(src, 1)],
            dst_ref=second.at[pl.ds(r0 + 1, rows), pl.ds(dst, 1)],
            send_sem=c_send.at[i, which], recv_sem=c_recv.at[i, which],
            device_id=(dev, row), device_id_type=MESH,
        )

    for a in range(3):
        weight(0, w1, wc1, a).wait()

    def pair(p, _):
        for q, first in ((0, 0), (1, 1), (2, 3)):

            @pl.when(p == first)
            def _():
                arrive(q)
                if q == 0:
                    field_up.start()
                if q == 2:
                    field_down.start()

        first_rows(1 + 2 * p, 2)
        side(p, 1 + 2 * p, 2, 0).start()
        side(p, 1 + 2 * p, 2, 1).start()
        return 0

    lax.fori_loop(0, PAIRS, pair, 0)

    edge = (
        (0, 0, H + 1, up),
        (H - 1, H + 1, 0, down),
    )

    def edge_copies(i):
        r, _, to, dev = edge[i]
        rows_copy = pltpu.make_async_remote_copy(
            src_ref=second.at[r + 1, pl.ds(1, W)], dst_ref=second.at[to, pl.ds(1, W)],
            send_sem=r_send.at[i], recv_sem=r_recv.at[i],
            device_id=(me, dev), device_id_type=MESH,
        )
        low = pltpu.make_async_remote_copy(
            src_ref=second.at[r + 1, pl.ds(1, 1)], dst_ref=second.at[to, pl.ds(W + 1, 1)],
            send_sem=d_send.at[i, 0], recv_sem=d_recv.at[i, 0],
            device_id=(left, dev), device_id_type=MESH,
        )
        high = pltpu.make_async_remote_copy(
            src_ref=second.at[r + 1, pl.ds(W, 1)], dst_ref=second.at[to, pl.ds(0, 1)],
            send_sem=d_send.at[i, 1], recv_sem=d_recv.at[i, 1],
            device_id=(right, dev), device_id_type=MESH,
        )
        return [rows_copy, low, high, side(PAIRS + i, r, 1, 0), side(PAIRS + i, r, 1, 1)]

    for i, arrival, missing in ((0, field_down, 0), (1, field_up, 7)):
        arrival.wait_recv()
        r, halo = edge[i][0], edge[i][1]

        @pl.when(row == missing)
        def _():
            field[halo] = jnp.zeros((WH, N, C), BF16)

        first_rows(r, 1)
        for copy in edge_copies(i):
            copy.start()

    for a in range(3):
        weight(1, w2, wc2, a).wait()

    def clear_sides(r0, rows):
        @pl.when(me == 0)
        def _():
            second[pl.ds(r0, rows), 0] = jnp.zeros((rows, N, C), BF16)

        @pl.when(me == N - 1)
        def _():
            second[pl.ds(r0, rows), W + 1] = jnp.zeros((rows, N, C), BF16)

    for p in range(PAIRS):
        for which in range(2):
            side(p, 1 + 2 * p, 2, which).wait_recv()
    clear_sides(2, H - 2)

    def out_copy(q, k):
        return pltpu.make_async_remote_copy(
            src_ref=ostage.at[q, peer(me, k)],
            dst_ref=out.at[me, q],
            send_sem=out_send.at[q, k],
            recv_sem=out_recv.at[q, k],
            device_id=(peer(me, k), row),
            device_id_type=MESH,
        )

    def out_arrival(q, k):
        return pltpu.make_async_remote_copy(
            src_ref=ostage.at[q, peer(me, k)],
            dst_ref=out.at[source(me, k), q],
            send_sem=out_send.at[q, k],
            recv_sem=out_recv.at[q, k],
            device_id=(peer(me, k), row),
            device_id_type=MESH,
        )

    def own_copy(q):
        return pltpu.make_async_copy(ostage.at[q, me], out.at[me, q], own_sem.at[q])

    def block(i, _):
        q = (i + 1) % QO

        @pl.when(i == 2)
        def _():
            for n in range(2):
                for copy in edge_copies(n):
                    copy.wait_recv()
            for n, missing in ((0, 7), (1, 0)):
                to = edge[n][2]

                @pl.when(row == missing)
                def _():
                    second[to] = jnp.zeros((WH, N, C), BF16)

            for r in (0, H):
                clear_sides(r, 2)

        multiply(second, wc2, q * RO, RO)

        def finish(px, _):
            v = collect(px, 1)[0] + b2[...].reshape(1, C)
            for lane in range(LANES):
                otr[lane, pl.ds(px, N, stride=PO)] = v[:, lane * 128 : (lane + 1) * 128]
            return 0

        lax.fori_loop(0, RO * W, finish, 0)

        def narrow(f, _):
            v = [otr[lane, pl.ds(f * PO, PO)] for lane in range(LANES)]
            ostage[q, f] = jnp.concatenate(v, axis=-1).astype(BF16)
            return 0

        lax.fori_loop(0, N, narrow, 0)
        for k in ORDER:
            out_copy(q, k).start()
        own_copy(q).start()
        return 0

    lax.fori_loop(0, QO, block, 0)

    for q in range(QO):
        for k in ORDER:
            out_arrival(q, k).wait_recv()
            out_copy(q, k).wait_send()
        own_copy(q).wait()
    for q in range(QI):
        for k in ORDER:
            in_copy(q, k).wait_send()
    field_up.wait_send()
    field_down.wait_send()
    for p in range(PAIRS):
        for which in range(2):
            side(p, 1 + 2 * p, 2, which).wait_send()
    for i in range(2):
        for copy in edge_copies(i):
            copy.wait_send()


def assemble(parts, lat, out, wide, line):
    for q in range(QO):
        for j in range(N):
            wide[j] = parts[j, q].astype(F32)
        for r in range(RO):
            for j in range(N):
                line[r, j * W : (j + 1) * W] = wide[j, r * W : (r + 1) * W]
            at = q * RO + r
            out[at] = (line[r] + lat[at].astype(F32)).astype(BF16)


def on_device(lat, g1, w1, b1, g2, w2, b2):
    lat = lat.reshape(H, COLS, C)
    vmem, hbm = pl.BlockSpec(memory_space=pltpu.VMEM), pl.BlockSpec(memory_space=pl.ANY)
    dma = pltpu.SemaphoreType.DMA
    parts = pl.pallas_call(
        kernel,
        out_shape=jax.ShapeDtypeStruct((N, QO, PO, C), BF16),
        in_specs=[vmem, vmem, hbm, vmem, vmem, hbm, vmem],
        out_specs=hbm,
        scratch_shapes=[
            pltpu.VMEM((9 * C, 3 * C), BF16),
            pltpu.VMEM((9 * C, 3 * C), BF16),
            pltpu.VMEM((H + 2, WH, N, C), BF16),
            pltpu.VMEM((H + 2, WH, N, C), BF16),
            pltpu.VMEM((QI, N, PI, C), BF16),
            pltpu.VMEM((QI, N, PI, C), BF16),
            pltpu.VMEM((H, COLS + 16, C), F32),
            pltpu.VMEM((4, PI, C), F32),
            pltpu.VMEM((LANES, N * PI, 128), F32),
            pltpu.VMEM((RO * W * N, 3 * C), F32),
            pltpu.VMEM((LANES, N * PO, 128), F32),
            pltpu.VMEM((QO, N, PO, C), BF16),
            dma((2, 3)),
            dma((QI, N)), dma((QI, N)),
            dma((2,)), dma((2,)),
            dma((PAIRS + 2, 2)), dma((PAIRS + 2, 2)),
            dma((2,)), dma((2,)),
            dma((2, 2)), dma((2, 2)),
            dma((QO, N)), dma((QO, N)),
            dma((QO,)),
        ],
        compiler_params=pltpu.CompilerParams(
            collective_id=0, has_side_effects=True, vmem_limit_bytes=60 << 20
        ),
        name="block",
    )(lat, g1, w1, b1, g2, w2, b2)
    result = pl.pallas_call(
        assemble,
        out_shape=jax.ShapeDtypeStruct((H, COLS, C), BF16),
        in_specs=[vmem, vmem],
        out_specs=vmem,
        scratch_shapes=[pltpu.VMEM((N, PO, C), F32), pltpu.VMEM((RO, COLS, C), F32)],
        compiler_params=pltpu.CompilerParams(vmem_limit_bytes=60 << 20),
        name="assemble",
    )(parts, lat)
    return result.reshape(1, H, COLS, C)


def solution(mesh):
    return jax.shard_map(
        on_device,
        mesh=mesh,
        in_specs=(P("tm", "rows", None, None), P(), P(), P(), P(), P(), P()),
        out_specs=P("tm", "rows", None, None),
        check_vma=False,
    )
```

```python
import functools

import jax
import jax.numpy as jnp
from jax import lax
from jax.experimental import pallas as pl
from jax.experimental.pallas import tpu as pltpu
from jax.sharding import PartitionSpec as P

MESH = pl.DeviceIdType.MESH
F32, BF16 = jnp.float32, jnp.bfloat16

C = 384
LANES = C // 128
H = 12
COLS = 160
N = 16
W = COLS // N
WH = W + 2
QI, RI = 3, 4
QO, RO = 4, 3
PI = RI * WH
PO = 32


def norm_act(v, gain):
    scale = lax.rsqrt(jnp.mean(v * v, axis=-1, keepdims=True) + 1e-06)
    u = v * scale * gain
    half = 0.5 * u
    return half + half * jnp.tanh(half)


def later(v, frames):
    at = lax.broadcasted_iota(jnp.int32, v.shape, v.ndim - 2)
    return jnp.where(at < frames, 0.0, pltpu.roll(v, frames, v.ndim - 2))


def peer(me, k):
    z, x, c = me // 8, (me // 2) % 4, me % 2
    dz, dx, dc = k // 8, (k // 2) % 4, k % 2
    return ((z + dz) % 2) * 8 + ((x + dx) % 4) * 2 + (c + dc) % 2


def source(me, k):
    z, x, c = me // 8, (me // 2) % 4, me % 2
    dz, dx, dc = k // 8, (k // 2) % 4, k % 2
    return ((z + dz) % 2) * 8 + ((x + 4 - dx) % 4) * 2 + (c + dc) % 2


ORDER = (12, 13, 4, 5, 10, 11, 14, 15, 2, 3, 6, 7, 8, 9, 1)


def kernel(
    lat_hbm, g1, w1, b1, g2, w2, b2,
    out,
    wc, act, recv, send, lat, nrm, pk, tr, prod, otr, ostage,
    w_sem, lat_sem, in_send, in_recv, f_send, f_recv, c_send, c_recv, r_send, r_recv,
    out_send, out_recv, own_sem,
):
    field, second = act.at[0], act.at[1]
    me = lax.axis_index("tm")
    row = lax.axis_index("rows")
    left, right = (me + N - 1) % N, (me + 1) % N
    up, down = (row + 7) % 8, (row + 1) % 8

    barrier = pltpu.get_barrier_semaphore()
    for dev in (up, down):
        pl.semaphore_signal(barrier, inc=1, device_id=(me, dev), device_id_type=MESH)
    for k in ORDER:
        pl.semaphore_signal(barrier, inc=1, device_id=(peer(me, k), row), device_id_type=MESH)

    lat_copy = pltpu.make_async_copy(lat_hbm, lat, lat_sem)
    lat_copy.start()

    def weight(i, a):
        return pltpu.make_async_copy(
            (w1, w2)[i].at[pl.ds(a * 9 * C, 9 * C)],
            wc.at[i, :, pl.ds((2 - a) * C, C)],
            w_sem.at[i, a],
        )

    for i in range(2):
        for a in range(3):
            weight(i, a).start()

    nrm[:, 0:8] = jnp.zeros((H, 8, C), F32)
    nrm[:, 8 + COLS : 16 + COLS] = jnp.zeros((H, 8, C), F32)
    otr[...] = jnp.zeros_like(otr)

    def in_copy(q, k):
        return pltpu.make_async_remote_copy(
            src_ref=send.at[q, peer(me, k)],
            dst_ref=recv.at[q, me],
            send_sem=in_send.at[q, k],
            recv_sem=in_recv.at[q, k],
            device_id=(peer(me, k), row),
            device_id_type=MESH,
        )

    def in_arrival(q, k):
        return pltpu.make_async_remote_copy(
            src_ref=send.at[q, peer(me, k)],
            dst_ref=recv.at[q, source(me, k)],
            send_sem=in_send.at[q, k],
            recv_sem=in_recv.at[q, k],
            device_id=(peer(me, k), row),
            device_id_type=MESH,
        )

    def norm_row(r, _):
        nrm[r, 8 : 8 + COLS] = norm_act(lat[r].astype(F32), g1[...].reshape(1, C))
        return 0

    def pack(q, _):
        for j in range(N):
            for n in range(RI):
                pk[j % 4, n * WH : (n + 1) * WH] = nrm[q * RI + n, j * W + 7 : j * W + 7 + WH]
            send[q, j] = pk[j % 4].astype(BF16)
        recv[q, me] = send[q, me]
        return 0

    def dispatch(q, _):
        for k in ORDER:
            in_copy(q, k).start()
        return 0

    lat_copy.wait()
    lax.fori_loop(0, H, norm_row, 0)
    lax.fori_loop(0, QI, pack, 0)
    pl.semaphore_wait(barrier, N - 1 + 2)
    lax.fori_loop(0, QI, dispatch, 0)

    def row_halo(i, ref, at, to, dev, columns, s_sem, r_sem):
        return pltpu.make_async_remote_copy(
            src_ref=ref.at[at, columns], dst_ref=ref.at[to, columns],
            send_sem=s_sem.at[i], recv_sem=r_sem.at[i],
            device_id=(me, dev), device_id_type=MESH,
        )

    every, own = pl.ds(0, WH), pl.ds(1, W)
    field_up = row_halo(0, field, 1, H + 1, up, every, f_send, f_recv)
    field_down = row_halo(1, field, H, 0, down, every, f_send, f_recv)

    def arrive(q):
        for k in ORDER:
            in_arrival(q, k).wait_recv()

        def widen(f, _):
            v = recv[q, f].astype(F32)
            for lane in range(LANES):
                tr[lane, pl.ds(f * PI, PI)] = v[:, lane * 128 : (lane + 1) * 128]
            return 0

        lax.fori_loop(0, N, widen, 0, unroll=4)
        for n in range(RI):

            def turn(c, _):
                v = [tr[lane, pl.ds(n * WH + c, N, stride=PI)] for lane in range(LANES)]
                field[1 + q * RI + n, c] = jnp.concatenate(v, axis=-1).astype(BF16)
                return 0

            lax.fori_loop(0, WH, turn, 0, unroll=True)

    def multiply(conv, rows):
        taps = [
            jnp.concatenate([act[conv, r + b, e : e + W] for r in rows], axis=0).reshape(-1, C)
            for b in range(3) for e in range(3)
        ]
        prod[...] = jnp.dot(
            jnp.concatenate(taps, axis=-1), wc[conv], preferred_element_type=F32
        )

    def collect(px, count):
        v = prod[pl.ds(px * N, count * N)].reshape(count, N, 3 * C)
        return v[:, :, :C] + later(v[:, :, C : 2 * C], 1) + later(v[:, :, 2 * C :], 2)

    def side(i, at, rows, which):
        src, dst, dev = ((1, W + 1, left), (W, 0, right))[which]
        return pltpu.make_async_remote_copy(
            src_ref=second.at[pl.ds(at, rows), pl.ds(src, 1)],
            dst_ref=second.at[pl.ds(at, rows), pl.ds(dst, 1)],
            send_sem=c_send.at[i, which], recv_sem=c_recv.at[i, which],
            device_id=(dev, row), device_id_type=MESH,
        )

    edges, halos = ((6, 1, 1), (7, H, 1)), ((8, 0, 1), (9, H + 1, 1))

    def start_sides(*which):
        for s in which:
            for n in range(2):
                side(*s, n).start()

    def await_sides(*which):
        for s in which:
            for n in range(2):
                side(*s, n).wait_recv()
            _, at, rows = s

            @pl.when(me == 0)
            def _():
                second[pl.ds(at, rows), 0] = jnp.zeros((rows, N, C), BF16)

            @pl.when(me == N - 1)
            def _():
                second[pl.ds(at, rows), W + 1] = jnp.zeros((rows, N, C), BF16)

    second_up = row_halo(0, second, 1, H + 1, up, own, r_send, r_recv)
    second_down = row_halo(1, second, H, 0, down, own, r_send, r_recv)

    def out_copy(q, k):
        return pltpu.make_async_remote_copy(
            src_ref=ostage.at[q, peer(me, k)],
            dst_ref=out.at[me, q],
            send_sem=out_send.at[q, k],
            recv_sem=out_recv.at[q, k],
            device_id=(peer(me, k), row),
            device_id_type=MESH,
        )

    def out_arrival(q, k):
        return pltpu.make_async_remote_copy(
            src_ref=ostage.at[q, peer(me, k)],
            dst_ref=out.at[source(me, k), q],
            send_sem=out_send.at[q, k],
            recv_sem=out_recv.at[q, k],
            device_id=(peer(me, k), row),
            device_id_type=MESH,
        )

    def own_copy(q):
        return pltpu.make_async_copy(ostage.at[q, me], out.at[me, q], own_sem.at[q])

    def finish_first(rows):
        for n, r in enumerate(rows):

            def some(g, _):
                v = collect(n * W + g * 2, 2) + b1[...].reshape(1, C)
                v = norm_act(v, g2[...].reshape(1, C))
                second[r + 1, pl.ds(1 + g * 2, 2)] = v.astype(BF16)
                return 0

            lax.fori_loop(0, W // 2, some, 0, unroll=True)

    def finish_second(rows):
        for n, r in enumerate(rows):

            def some(c, _):
                v = collect(n * W + c, 1)[0] + b2[...].reshape(1, C)
                px = (r // RO) * PO + (r % RO) * W + c
                for lane in range(LANES):
                    otr[lane, pl.ds(px, N, stride=QO * PO)] = v[:, lane * 128 : (lane + 1) * 128]
                return 0

            lax.fori_loop(0, W, some, 0, unroll=True)

    def give(q):
        def narrow(f, _):
            v = [otr[lane, pl.ds((f * QO + q) * PO, PO)] for lane in range(LANES)]
            ostage[q, f] = jnp.concatenate(v, axis=-1).astype(BF16)
            return 0

        lax.fori_loop(0, N, narrow, 0, unroll=4)
        for k in ORDER:
            out_copy(q, k).start()
        own_copy(q).start()

    def clear(ref, at, missing, low, high):
        @pl.when(row == missing)
        def _():
            ref[at, low:high] = jnp.zeros((high - low, N, C), BF16)

    def pair(i):
        return (i, 2 * i + 2, 2)

    def step(i, _):
        conv = jnp.where((i < 5) | (i == 6), 0, 1)

        @pl.when((i == 0) | (i == 1) | (i == 3))
        def _():
            arrive(i - i // 3)

        @pl.when(i == 0)
        def _():
            field_up.start()
            for a in range(3):
                weight(0, a).wait()

        @pl.when(i == 3)
        def _():
            field_down.start()

        @pl.when(i == 6)
        def _():
            field_down.wait_recv()
            clear(field, 0, 0, 0, WH)
            field_up.wait_recv()
            clear(field, H + 1, 7, 0, WH)

        @pl.when(i == 5)
        def _():
            for a in range(3):
                weight(1, a).wait()
            await_sides(pair(0), pair(1))

        @pl.when((i >= 7) & (i <= 9))
        def _():
            await_sides(pair(i - 5))

        @pl.when(i == 9)
        def _():
            second_down.wait_recv()
            clear(second, 0, 0, 1, 1 + W)
            second_up.wait_recv()
            clear(second, H + 1, 7, 1, 1 + W)
            start_sides(*halos)

        @pl.when(i == 10)
        def _():
            await_sides(edges[0], halos[0])

        @pl.when(i == 11)
        def _():
            await_sides(edges[1], halos[1])

        low = jnp.where(i < 5, 2 * i + 1, jnp.where(i == 5, 2, jnp.where(i == 11, 10, 2 * i - 10)))
        low = jnp.where((i == 6) | (i == 10), 0, low)
        high = jnp.where(i == 6, 11, low + 1)
        multiply(conv, (low, high))

        @pl.when(conv == 0)
        def _():
            finish_first((low, high))

        @pl.when(i == 6)
        def _():
            second_up.start()
            second_down.start()
            start_sides(*edges)

        @pl.when(i < 5)
        def _():
            start_sides(pair(i))

        @pl.when(conv == 1)
        def _():
            finish_second((low, high))

        @pl.when((i == 7) | (i >= 9))
        def _():
            give(jnp.where(i == 10, 0, (i - 5) // 2))

        return 0

    lax.fori_loop(0, 12, step, 0)

    def drain_in(q, _):
        for k in ORDER:
            in_copy(q, k).wait_send()
        return 0

    lax.fori_loop(0, QI, drain_in, 0)
    for copy in (field_up, field_down, second_up, second_down):
        copy.wait_send()
    for s in [pair(i) for i in range(5)] + list(edges + halos):
        for n in range(2):
            side(*s, n).wait_send()

    def drain_out(q, _):
        for k in ORDER:
            out_arrival(q, k).wait_recv()
            out_copy(q, k).wait_send()
        own_copy(q).wait()
        return 0

    lax.fori_loop(0, QO, drain_out, 0)


def assemble(parts, lat, out, wide, line):
    for j in range(N):
        wide[j] = parts[j, 0].astype(F32)
    for r in range(RO):
        for j in range(N):
            line[r, j * W : (j + 1) * W] = wide[j, r * W : (r + 1) * W]
        out[r] = (line[r] + lat[r].astype(F32)).astype(BF16)


def on_device(lat, g1, w1, b1, g2, w2, b2):
    lat = lat.reshape(H, COLS, C)
    vmem, hbm = pl.BlockSpec(memory_space=pltpu.VMEM), pl.BlockSpec(memory_space=pl.ANY)
    dma = pltpu.SemaphoreType.DMA
    parts = pl.pallas_call(
        kernel,
        out_shape=jax.ShapeDtypeStruct((N, QO, PO, C), BF16),
        in_specs=[hbm, vmem, hbm, vmem, vmem, hbm, vmem],
        out_specs=hbm,
        scratch_shapes=[
            pltpu.VMEM((2, 9 * C, 3 * C), BF16),
            pltpu.VMEM((2, H + 2, WH, N, C), BF16),
            pltpu.VMEM((QI, N, PI, C), BF16),
            pltpu.VMEM((QI, N, PI, C), BF16),
            pltpu.VMEM((H, COLS, C), BF16),
            pltpu.VMEM((H, COLS + 16, C), F32),
            pltpu.VMEM((4, PI, C), F32),
            pltpu.VMEM((LANES, N * PI, 128), F32),
            pltpu.VMEM((2 * W * N, 3 * C), F32),
            pltpu.VMEM((LANES, N * QO * PO, 128), F32),
            pltpu.VMEM((QO, N, PO, C), BF16),
            dma((2, 3)), dma,
            dma((QI, N)), dma((QI, N)),
            dma((2,)), dma((2,)),
            dma((10, 2)), dma((10, 2)),
            dma((2,)), dma((2,)),
            dma((QO, N)), dma((QO, N)),
            dma((QO,)),
        ],
        compiler_params=pltpu.CompilerParams(
            collective_id=0, has_side_effects=True, vmem_limit_bytes=60 << 20
        ),
        name="block",
    )(lat, g1, w1, b1, g2, w2, b2)
    result = pl.pallas_call(
        assemble,
        out_shape=jax.ShapeDtypeStruct((H, COLS, C), BF16),
        grid=(QO,),
        in_specs=[
            pl.BlockSpec((N, 1, PO, C), lambda q: (0, q, 0, 0)),
            pl.BlockSpec((RO, COLS, C), lambda q: (q, 0, 0)),
        ],
        out_specs=pl.BlockSpec((RO, COLS, C), lambda q: (q, 0, 0)),
        scratch_shapes=[pltpu.VMEM((N, PO, C), F32), pltpu.VMEM((RO, COLS, C), F32)],
        compiler_params=pltpu.CompilerParams(vmem_limit_bytes=32 << 20),
        name="assemble",
    )(parts, lat)
    return result.reshape(1, H, COLS, C)


def solution(mesh):
    return jax.shard_map(
        on_device,
        mesh=mesh,
        in_specs=(P("tm", "rows", None, None), P(), P(), P(), P(), P(), P()),
        out_specs=P("tm", "rows", None, None),
        check_vma=False,
    )
```

```python
import functools

import jax
import jax.numpy as jnp
from jax import lax
from jax.experimental import pallas as pl
from jax.experimental.pallas import tpu as pltpu
from jax.sharding import PartitionSpec as P

MESH = pl.DeviceIdType.MESH
F32, BF16 = jnp.float32, jnp.bfloat16

C = 384
LANES = C // 128
H = 12
COLS = 160
N = 16
W = COLS // N
WH = W + 2
QI, RI = 3, 4
QO, RO = 4, 3
OUT_FROM = 2
PI = RI * WH
PO = 32


def norm_act(v, gain):
    scale = lax.rsqrt(jnp.mean(v * v, axis=-1, keepdims=True) + 1e-06)
    u = v * scale * gain
    half = 0.5 * u
    return half + half * jnp.tanh(half)


def later(v, frames):
    at = lax.broadcasted_iota(jnp.int32, v.shape, v.ndim - 2)
    return jnp.where(at < frames, 0.0, pltpu.roll(v, frames, v.ndim - 2))


def peer(me, k):
    z, x, c = me // 8, (me // 2) % 4, me % 2
    dz, dx, dc = k // 8, (k // 2) % 4, k % 2
    return ((z + dz) % 2) * 8 + ((x + dx) % 4) * 2 + (c + dc) % 2


def source(me, k):
    z, x, c = me // 8, (me // 2) % 4, me % 2
    dz, dx, dc = k // 8, (k // 2) % 4, k % 2
    return ((z + dz) % 2) * 8 + ((x + 4 - dx) % 4) * 2 + (c + dc) % 2


ORDER = (12, 13, 4, 5, 10, 11, 14, 15, 2, 3, 6, 7, 8, 9, 1)


def kernel(
    lat_hbm, g1, w1, b1, g2, w2, b2,
    out,
    wc, act, recv, send, lat, nrm, pk, tr, prod, otr, ostage,
    w_sem, lat_sem, in_send, in_recv, f_send, f_recv, c_send, c_recv, r_send, r_recv, k_send, k_recv,
    out_send, out_recv, own_sem,
):
    field, second = act.at[0], act.at[1]
    me = lax.axis_index("tm")
    row = lax.axis_index("rows")
    left, right = (me + N - 1) % N, (me + 1) % N
    up, down = (row + 7) % 8, (row + 1) % 8
    to = {k: peer(me, k) for k in ORDER}
    source_of = {k: source(me, k) for k in ORDER}

    barrier = pltpu.get_barrier_semaphore()
    for dev in (up, down):
        pl.semaphore_signal(barrier, inc=1, device_id=(me, dev), device_id_type=MESH)
    for k in ORDER:
        pl.semaphore_signal(barrier, inc=1, device_id=(to[k], row), device_id_type=MESH)

    lat_copy = pltpu.make_async_copy(lat_hbm, lat, lat_sem)
    lat_copy.start()

    def weight(i, a):
        return pltpu.make_async_copy(
            (w1, w2)[i].at[pl.ds(a * 9 * C, 9 * C)],
            wc.at[i, :, pl.ds((2 - a) * C, C)],
            w_sem.at[i, a],
        )

    for i in range(2):
        for a in range(3):
            weight(i, a).start()

    nrm[:, 0:8] = jnp.zeros((H, 8, C), F32)
    nrm[:, 8 + COLS : 16 + COLS] = jnp.zeros((H, 8, C), F32)
    otr[...] = jnp.zeros_like(otr)

    def in_copy(q, k):
        return pltpu.make_async_remote_copy(
            src_ref=send.at[q, to[k]],
            dst_ref=recv.at[q, me],
            send_sem=in_send.at[q, k],
            recv_sem=in_recv.at[q, k],
            device_id=(to[k], row),
            device_id_type=MESH,
        )

    def in_arrival(q, k):
        return pltpu.make_async_remote_copy(
            src_ref=send.at[q, to[k]],
            dst_ref=recv.at[q, source_of[k]],
            send_sem=in_send.at[q, k],
            recv_sem=in_recv.at[q, k],
            device_id=(to[k], row),
            device_id_type=MESH,
        )

    def norm_row(r, _):
        nrm[r, 8 : 8 + COLS] = norm_act(lat[r].astype(F32), g1[...].reshape(1, C))
        return 0

    def pack(q, _):
        for j in range(N):
            for n in range(RI):
                pk[j % 4, n * WH : (n + 1) * WH] = nrm[q * RI + n, j * W + 7 : j * W + 7 + WH]
            send[q, j] = pk[j % 4].astype(BF16)
        recv[q, me] = send[q, me]
        return 0

    def dispatch(q, _):
        for k in ORDER:
            in_copy(q, k).start()
        return 0

    lat_copy.wait()
    lax.fori_loop(0, H, norm_row, 0)
    lax.fori_loop(0, QI, pack, 0)
    pl.semaphore_wait(barrier, N - 1 + 2)
    lax.fori_loop(0, QI, dispatch, 0)

    def row_halo(i, ref, at, target, dev, columns, s_sem, r_sem):
        return pltpu.make_async_remote_copy(
            src_ref=ref.at[at, columns], dst_ref=ref.at[target, columns],
            send_sem=s_sem.at[i], recv_sem=r_sem.at[i],
            device_id=(me, dev), device_id_type=MESH,
        )

    every, own = pl.ds(0, WH), pl.ds(1, W)
    field_up = row_halo(0, field, 1, H + 1, up, every, f_send, f_recv)
    field_down = row_halo(1, field, H, 0, down, every, f_send, f_recv)

    def arrive(q):
        for k in ORDER:
            in_arrival(q, k).wait_recv()

        def widen(f, _):
            v = recv[q, f].astype(F32)
            for lane in range(LANES):
                tr[lane, pl.ds(f * PI, PI)] = v[:, lane * 128 : (lane + 1) * 128]
            return 0

        lax.fori_loop(0, N, widen, 0, unroll=4)
        for n in range(RI):

            def turn(c, _):
                v = [tr[lane, pl.ds(n * WH + c, N, stride=PI)] for lane in range(LANES)]
                field[1 + q * RI + n, c] = jnp.concatenate(v, axis=-1).astype(BF16)
                return 0

            lax.fori_loop(0, WH, turn, 0, unroll=True)

    def multiply(conv, rows):
        taps = [
            jnp.concatenate([act[conv, r + b, e : e + W] for r in rows], axis=0).reshape(-1, C)
            for b in range(3) for e in range(3)
        ]
        prod[...] = jnp.dot(
            jnp.concatenate(taps, axis=-1), wc[conv], preferred_element_type=F32
        )

    def collect(px, count):
        v = prod[pl.ds(px * N, count * N)].reshape(count, N, 3 * C)
        return v[:, :, :C] + later(v[:, :, C : 2 * C], 1) + later(v[:, :, 2 * C :], 2)

    def side(i, at, rows, which):
        src, dst, dev = ((1, W + 1, left), (W, 0, right))[which]
        return pltpu.make_async_remote_copy(
            src_ref=second.at[pl.ds(at, rows), pl.ds(src, 1)],
            dst_ref=second.at[pl.ds(at, rows), pl.ds(dst, 1)],
            send_sem=c_send.at[i, which], recv_sem=c_recv.at[i, which],
            device_id=(dev, row), device_id_type=MESH,
        )

    edges = ((5, 1, 1), (6, H, 1))

    def pair(p):
        return (p, 2 * p + 2, 2)

    def start_sides(*which):
        for s in which:
            for n in range(2):
                side(*s, n).start()

    def await_sides(*which):
        for s in which:
            for n in range(2):
                side(*s, n).wait_recv()
            _, at, rows = s

            @pl.when(me == 0)
            def _():
                second[pl.ds(at, rows), 0] = jnp.zeros((rows, N, C), BF16)

            @pl.when(me == N - 1)
            def _():
                second[pl.ds(at, rows), W + 1] = jnp.zeros((rows, N, C), BF16)

    corners = []
    for i, (at, target, dev) in enumerate(((1, H + 1, up), (H, 0, down))):
        corners.append([
            row_halo(n, second, at, target, dev, pl.ds(column, 1), k_send.at[i], k_recv.at[i])
            for n, column in enumerate((0, W + 1))
        ])

    second_up = row_halo(0, second, 1, H + 1, up, own, r_send, r_recv)
    second_down = row_halo(1, second, H, 0, down, own, r_send, r_recv)

    def out_copy(q, k):
        return pltpu.make_async_remote_copy(
            src_ref=ostage.at[q, to[k]],
            dst_ref=out.at[me, q],
            send_sem=out_send.at[q, k],
            recv_sem=out_recv.at[q, k],
            device_id=(to[k], row),
            device_id_type=MESH,
        )

    def out_arrival(q, k):
        return pltpu.make_async_remote_copy(
            src_ref=ostage.at[q, to[k]],
            dst_ref=out.at[source_of[k], q],
            send_sem=out_send.at[q, k],
            recv_sem=out_recv.at[q, k],
            device_id=(to[k], row),
            device_id_type=MESH,
        )

    def own_copy(q):
        return pltpu.make_async_copy(ostage.at[q, me], out.at[me, q], own_sem.at[q])

    def finish_first(rows):
        for n, r in enumerate(rows):

            def some(g, _):
                v = collect(n * W + g * 2, 2) + b1[...].reshape(1, C)
                v = norm_act(v, g2[...].reshape(1, C))
                second[r + 1, pl.ds(1 + g * 2, 2)] = v.astype(BF16)
                return 0

            lax.fori_loop(0, W // 2, some, 0, unroll=True)

    def finish_second(rows):
        for n, r in enumerate(rows):

            def some(c, _):
                v = collect(n * W + c, 1)[0] + b2[...].reshape(1, C)
                slot = (r + H - OUT_FROM) % H
                px = (slot // RO) * PO + (slot % RO) * W + c
                for lane in range(LANES):
                    otr[lane, pl.ds(px, N, stride=QO * PO)] = v[:, lane * 128 : (lane + 1) * 128]
                return 0

            lax.fori_loop(0, W, some, 0, unroll=True)

    def give(q):
        def narrow(f, _):
            v = [otr[lane, pl.ds((f * QO + q) * PO, PO)] for lane in range(LANES)]
            ostage[q, f] = jnp.concatenate(v, axis=-1).astype(BF16)
            return 0

        lax.fori_loop(0, N, narrow, 0, unroll=4)
        for k in ORDER:
            out_copy(q, k).start()
        own_copy(q).start()

    def clear(ref, at, missing):
        @pl.when(row == missing)
        def _():
            ref[at] = jnp.zeros((WH, N, C), BF16)

    def table(i, values):
        value = values[0]
        for n in range(1, len(values)):
            value = jnp.where(i == n, values[n], value)
        return value

    def step(i, _):
        conv = table(i, (0, 0, 0, 0, 0, 1, 0, 1, 1, 1, 1, 1))
        low = table(i, (1, 3, 5, 7, 9, 2, 0, 4, 6, 8, 1, 0))
        high = table(i, (2, 4, 6, 8, 10, 3, 11, 5, 7, 9, 10, 11))

        @pl.when((i == 0) | (i == 1) | (i == 3))
        def _():
            arrive(i - i // 3)

        @pl.when(i == 0)
        def _():
            for a in range(3):
                weight(0, a).wait()

        @pl.when(i == 3)
        def _():
            field_down.start()
            field_up.start()

        @pl.when(i == 5)
        def _():
            for a in range(3):
                weight(1, a).wait()
            await_sides(pair(0), pair(1))

        @pl.when(i == 6)
        def _():
            field_down.wait_recv()
            clear(field, 0, 0)
            field_up.wait_recv()
            clear(field, H + 1, 7)

        @pl.when((i >= 7) & (i <= 9))
        def _():
            await_sides(pair(i - 5))

        @pl.when(i == 11)
        def _():
            for copy in [second_down, second_up] + corners[0] + corners[1]:
                copy.wait_recv()
            clear(second, 0, 0)
            clear(second, H + 1, 7)

        multiply(conv, (low, high))

        @pl.when(conv == 0)
        def _():
            finish_first((low, high))

        @pl.when(i == 6)
        def _():
            second_up.start()
            second_down.start()
            start_sides(*edges)

        @pl.when(i < 5)
        def _():
            start_sides(pair(i))

        @pl.when(i == 8)
        def _():
            await_sides(*edges)
            for copy in corners[0] + corners[1]:
                copy.start()

        @pl.when(conv == 1)
        def _():
            finish_second((low, high))

        @pl.when((i == 7) | (i == 8) | (i >= 10))
        def _():
            give(i - 7 - i // 10)

        return 0

    lax.fori_loop(0, 12, step, 0)

    def drain_in(q, _):
        for k in ORDER:
            in_copy(q, k).wait_send()
        return 0

    lax.fori_loop(0, QI, drain_in, 0)
    for copy in [field_up, field_down, second_up, second_down] + corners[0] + corners[1]:
        copy.wait_send()
    for s in [pair(p) for p in range(5)] + list(edges):
        for n in range(2):
            side(*s, n).wait_send()

    def drain_out(q, _):
        for k in ORDER:
            out_arrival(q, k).wait_recv()
            out_copy(q, k).wait_send()
        own_copy(q).wait()
        return 0

    lax.fori_loop(0, QO, drain_out, 0)


def assemble(parts, lat, out, wide, line):
    q = pl.program_id(0)
    for j in range(N):
        wide[j] = parts[j, 0].astype(F32)
    for r in range(RO):
        for j in range(N):
            line[r, j * W : (j + 1) * W] = wide[j, r * W : (r + 1) * W]
        at = (q * RO + r + OUT_FROM) % H
        out[at] = (line[r] + lat[at].astype(F32)).astype(BF16)


def on_device(lat, g1, w1, b1, g2, w2, b2):
    lat = lat.reshape(H, COLS, C)
    vmem, hbm = pl.BlockSpec(memory_space=pltpu.VMEM), pl.BlockSpec(memory_space=pl.ANY)
    dma = pltpu.SemaphoreType.DMA
    parts = pl.pallas_call(
        kernel,
        out_shape=jax.ShapeDtypeStruct((N, QO, PO, C), BF16),
        in_specs=[hbm, vmem, hbm, vmem, vmem, hbm, vmem],
        out_specs=hbm,
        scratch_shapes=[
            pltpu.VMEM((2, 9 * C, 3 * C), BF16),
            pltpu.VMEM((2, H + 2, WH, N, C), BF16),
            pltpu.VMEM((QI, N, PI, C), BF16),
            pltpu.VMEM((QI, N, PI, C), BF16),
            pltpu.VMEM((H, COLS, C), BF16),
            pltpu.VMEM((H, COLS + 16, C), F32),
            pltpu.VMEM((4, PI, C), F32),
            pltpu.VMEM((LANES, N * PI, 128), F32),
            pltpu.VMEM((2 * W * N, 3 * C), F32),
            pltpu.VMEM((LANES, N * QO * PO, 128), F32),
            pltpu.VMEM((QO, N, PO, C), BF16),
            dma((2, 3)), dma,
            dma((QI, N)), dma((QI, N)),
            dma((2,)), dma((2,)),
            dma((7, 2)), dma((7, 2)),
            dma((2,)), dma((2,)),
            dma((2, 2)), dma((2, 2)),
            dma((QO, N)), dma((QO, N)),
            dma((QO,)),
        ],
        compiler_params=pltpu.CompilerParams(
            collective_id=0, has_side_effects=True, vmem_limit_bytes=60 << 20
        ),
        name="block",
    )(lat, g1, w1, b1, g2, w2, b2)
    result = pl.pallas_call(
        assemble,
        out_shape=jax.ShapeDtypeStruct((H, COLS, C), BF16),
        grid=(QO,),
        in_specs=[
            pl.BlockSpec((N, 1, PO, C), lambda q: (0, q, 0, 0)),
            pl.BlockSpec((H, COLS, C), lambda q: (0, 0, 0)),
        ],
        out_specs=pl.BlockSpec((H, COLS, C), lambda q: (0, 0, 0)),
        scratch_shapes=[pltpu.VMEM((N, PO, C), F32), pltpu.VMEM((RO, COLS, C), F32)],
        compiler_params=pltpu.CompilerParams(vmem_limit_bytes=32 << 20),
        name="assemble",
    )(parts, lat)
    return result.reshape(1, H, COLS, C)


def solution(mesh):
    return jax.shard_map(
        on_device,
        mesh=mesh,
        in_specs=(P("tm", "rows", None, None), P(), P(), P(), P(), P(), P()),
        out_specs=P("tm", "rows", None, None),
        check_vma=False,
    )
```

```python
import functools

import jax
import jax.numpy as jnp
from jax import lax
from jax.experimental import pallas as pl
from jax.experimental.pallas import tpu as pltpu
from jax.sharding import PartitionSpec as P

MESH = pl.DeviceIdType.MESH
F32, BF16 = jnp.float32, jnp.bfloat16

C = 384
LANES = C // 128
H = 12
COLS = 160
N = 16
W = COLS // N
WH = W + 2
QI, RI = 3, 4
QO, RO = 4, 3
OUT_FROM = 2
PI = RI * WH
PO = 32


def norm_act(v, gain):
    scale = lax.rsqrt(jnp.mean(v * v, axis=-1, keepdims=True) + 1e-06)
    u = v * scale * gain
    half = 0.5 * u
    return half + half * jnp.tanh(half)


def later(v, frames):
    at = lax.broadcasted_iota(jnp.int32, v.shape, v.ndim - 2)
    return jnp.where(at < frames, 0.0, pltpu.roll(v, frames, v.ndim - 2))


def peer(me, k):
    z, x, c = me // 8, (me // 2) % 4, me % 2
    dz, dx, dc = k // 8, (k // 2) % 4, k % 2
    return ((z + dz) % 2) * 8 + ((x + dx) % 4) * 2 + (c + dc) % 2


def source(me, k):
    z, x, c = me // 8, (me // 2) % 4, me % 2
    dz, dx, dc = k // 8, (k // 2) % 4, k % 2
    return ((z + dz) % 2) * 8 + ((x + 4 - dx) % 4) * 2 + (c + dc) % 2


ORDER = (12, 13, 4, 5, 10, 11, 14, 15, 2, 3, 6, 7, 8, 9, 1)


def kernel(
    lat_hbm, g1, w1, b1, g2, w2, b2,
    out,
    wc, act, recv, send, lat, nrm, pk, tr, prod, otr, ostage,
    w_sem, lat_sem, in_send, in_recv, f_send, f_recv, c_send, c_recv, r_send, r_recv, k_send, k_recv,
    out_send, out_recv, own_sem,
):
    field, second = act.at[0], act.at[1]
    me = lax.axis_index("tm")
    row = lax.axis_index("rows")
    left, right = (me + N - 1) % N, (me + 1) % N
    up, down = (row + 7) % 8, (row + 1) % 8
    to = {k: peer(me, k) for k in ORDER}
    source_of = {k: source(me, k) for k in ORDER}

    barrier = pltpu.get_barrier_semaphore()
    for dev in (up, down):
        pl.semaphore_signal(barrier, inc=1, device_id=(me, dev), device_id_type=MESH)
    for k in ORDER:
        pl.semaphore_signal(barrier, inc=1, device_id=(to[k], row), device_id_type=MESH)

    lat_copy = pltpu.make_async_copy(lat_hbm, lat, lat_sem)
    lat_copy.start()

    def weight(i, a):
        return pltpu.make_async_copy(
            (w1, w2)[i].at[pl.ds(a * 9 * C, 9 * C)],
            wc.at[i, :, pl.ds((2 - a) * C, C)],
            w_sem.at[i, a],
        )

    for i in range(2):
        for a in range(3):
            weight(i, a).start()

    nrm[:, 0:8] = jnp.zeros((H, 8, C), F32)
    nrm[:, 8 + COLS : 16 + COLS] = jnp.zeros((H, 8, C), F32)
    otr[...] = jnp.zeros_like(otr)

    def in_copy(q, k):
        return pltpu.make_async_remote_copy(
            src_ref=send.at[q, to[k]],
            dst_ref=recv.at[q, me],
            send_sem=in_send.at[q, k],
            recv_sem=in_recv.at[q, k],
            device_id=(to[k], row),
            device_id_type=MESH,
        )

    def in_arrival(q, k):
        return pltpu.make_async_remote_copy(
            src_ref=send.at[q, to[k]],
            dst_ref=recv.at[q, source_of[k]],
            send_sem=in_send.at[q, k],
            recv_sem=in_recv.at[q, k],
            device_id=(to[k], row),
            device_id_type=MESH,
        )

    def norm_row(r, _):
        nrm[r, 8 : 8 + COLS] = norm_act(lat[r].astype(F32), g1[...].reshape(1, C))
        return 0

    def pack(q, _):
        for j in range(N):
            for n in range(RI):
                pk[j % 4, n * WH : (n + 1) * WH] = nrm[q * RI + n, j * W + 7 : j * W + 7 + WH]
            send[q, j] = pk[j % 4].astype(BF16)
        recv[q, me] = send[q, me]
        return 0

    def dispatch(q, _):
        for k in ORDER:
            in_copy(q, k).start()
        return 0

    lat_copy.wait()
    def ready(q, _):
        lax.fori_loop(q * RI, (q + 1) * RI, norm_row, 0)
        return pack(q, 0)

    ready(0, 0)
    pl.semaphore_wait(barrier, N - 1 + 2)
    dispatch(0, 0)

    def follow(q, _):
        ready(q, 0)
        return dispatch(q, 0)

    lax.fori_loop(1, QI, follow, 0)

    def row_halo(i, ref, at, target, dev, columns, s_sem, r_sem):
        return pltpu.make_async_remote_copy(
            src_ref=ref.at[at, columns], dst_ref=ref.at[target, columns],
            send_sem=s_sem.at[i], recv_sem=r_sem.at[i],
            device_id=(me, dev), device_id_type=MESH,
        )

    every, own = pl.ds(0, WH), pl.ds(1, W)
    field_up = row_halo(0, field, 1, H + 1, up, every, f_send, f_recv)
    field_down = row_halo(1, field, H, 0, down, every, f_send, f_recv)

    def arrive(q):
        for k in ORDER:
            in_arrival(q, k).wait_recv()

        def widen(f, _):
            v = recv[q, f].astype(F32)
            for lane in range(LANES):
                tr[lane, pl.ds(f * PI, PI)] = v[:, lane * 128 : (lane + 1) * 128]
            return 0

        lax.fori_loop(0, N, widen, 0, unroll=4)
        for n in (3, 0, 1, 2):

            def turn(c, _):
                v = [tr[lane, pl.ds(n * WH + c, N, stride=PI)] for lane in range(LANES)]
                field[1 + q * RI + n, c] = jnp.concatenate(v, axis=-1).astype(BF16)
                return 0

            lax.fori_loop(0, WH, turn, 0, unroll=True)
            if n == 3:

                @pl.when(q == QI - 1)
                def _():
                    field_down.start()
                    field_up.start()


    def multiply(conv, rows):
        taps = [
            jnp.concatenate([act[conv, r + b, e : e + W] for r in rows], axis=0).reshape(-1, C)
            for b in range(3) for e in range(3)
        ]
        prod[...] = jnp.dot(
            jnp.concatenate(taps, axis=-1), wc[conv], preferred_element_type=F32
        )

    def collect(px, count):
        v = prod[pl.ds(px * N, count * N)].reshape(count, N, 3 * C)
        return v[:, :, :C] + later(v[:, :, C : 2 * C], 1) + later(v[:, :, 2 * C :], 2)

    def side(i, at, rows, which):
        src, dst, dev = ((1, W + 1, left), (W, 0, right))[which]
        return pltpu.make_async_remote_copy(
            src_ref=second.at[pl.ds(at, rows), pl.ds(src, 1)],
            dst_ref=second.at[pl.ds(at, rows), pl.ds(dst, 1)],
            send_sem=c_send.at[i, which], recv_sem=c_recv.at[i, which],
            device_id=(dev, row), device_id_type=MESH,
        )

    edges = ((5, 1, 1), (6, H, 1))

    def pair(p):
        return (p, 2 * p + 2, 2)

    def start_sides(*which):
        for s in which:
            for n in range(2):
                side(*s, n).start()

    def await_sides(*which):
        for s in which:
            for n in range(2):
                side(*s, n).wait_recv()
            _, at, rows = s

            @pl.when(me == 0)
            def _():
                second[pl.ds(at, rows), 0] = jnp.zeros((rows, N, C), BF16)

            @pl.when(me == N - 1)
            def _():
                second[pl.ds(at, rows), W + 1] = jnp.zeros((rows, N, C), BF16)

    corners = []
    for i, (at, target, dev) in enumerate(((1, H + 1, up), (H, 0, down))):
        corners.append([
            row_halo(n, second, at, target, dev, pl.ds(column, 1), k_send.at[i], k_recv.at[i])
            for n, column in enumerate((0, W + 1))
        ])

    second_up = row_halo(0, second, 1, H + 1, up, own, r_send, r_recv)
    second_down = row_halo(1, second, H, 0, down, own, r_send, r_recv)

    def out_copy(q, k):
        return pltpu.make_async_remote_copy(
            src_ref=ostage.at[q, to[k]],
            dst_ref=out.at[me, q],
            send_sem=out_send.at[q, k],
            recv_sem=out_recv.at[q, k],
            device_id=(to[k], row),
            device_id_type=MESH,
        )

    def out_arrival(q, k):
        return pltpu.make_async_remote_copy(
            src_ref=ostage.at[q, to[k]],
            dst_ref=out.at[source_of[k], q],
            send_sem=out_send.at[q, k],
            recv_sem=out_recv.at[q, k],
            device_id=(to[k], row),
            device_id_type=MESH,
        )

    def own_copy(q):
        return pltpu.make_async_copy(ostage.at[q, me], out.at[me, q], own_sem.at[q])

    def finish_first(rows):
        for n, r in enumerate(rows):

            def some(g, _):
                v = collect(n * W + g * 2, 2) + b1[...].reshape(1, C)
                v = norm_act(v, g2[...].reshape(1, C))
                second[r + 1, pl.ds(1 + g * 2, 2)] = v.astype(BF16)
                return 0

            lax.fori_loop(0, W // 2, some, 0, unroll=True)

    def finish_second(rows):
        for n, r in enumerate(rows):

            def some(c, _):
                v = collect(n * W + c, 1)[0] + b2[...].reshape(1, C)
                slot = (r + H - OUT_FROM) % H
                px = (slot // RO) * PO + (slot % RO) * W + c
                for lane in range(LANES):
                    otr[lane, pl.ds(px, N, stride=QO * PO)] = v[:, lane * 128 : (lane + 1) * 128]
                return 0

            lax.fori_loop(0, W, some, 0, unroll=True)

    def give(q):
        def narrow(f, _):
            v = [otr[lane, pl.ds((f * QO + q) * PO, PO)] for lane in range(LANES)]
            ostage[q, f] = jnp.concatenate(v, axis=-1).astype(BF16)
            return 0

        lax.fori_loop(0, N, narrow, 0, unroll=4)
        for k in ORDER:
            out_copy(q, k).start()
        own_copy(q).start()

    def clear(ref, at, missing):
        @pl.when(row == missing)
        def _():
            ref[at] = jnp.zeros((WH, N, C), BF16)

    def table(i, values):
        value = values[0]
        for n in range(1, len(values)):
            value = jnp.where(i == n, values[n], value)
        return value

    def step(i, _):
        conv = table(i, (0, 0, 0, 0, 0, 1, 0, 1, 1, 1, 1, 1))
        low = table(i, (1, 3, 5, 7, 9, 2, 0, 4, 6, 8, 1, 0))
        high = table(i, (2, 4, 6, 8, 10, 3, 11, 5, 7, 9, 10, 11))

        @pl.when((i == 0) | (i == 1) | (i == 3))
        def _():
            arrive(i - i // 3)

        @pl.when(i == 0)
        def _():
            for a in range(3):
                weight(0, a).wait()

        @pl.when(i == 5)
        def _():
            for a in range(3):
                weight(1, a).wait()
            await_sides(pair(0), pair(1))

        @pl.when(i == 6)
        def _():
            field_down.wait_recv()
            clear(field, 0, 0)
            field_up.wait_recv()
            clear(field, H + 1, 7)

        @pl.when((i >= 7) & (i <= 9))
        def _():
            await_sides(pair(i - 5))

        @pl.when(i == 11)
        def _():
            for copy in [second_down, second_up] + corners[0] + corners[1]:
                copy.wait_recv()
            clear(second, 0, 0)
            clear(second, H + 1, 7)

        multiply(conv, (low, high))

        @pl.when(conv == 0)
        def _():
            finish_first((low, high))

        @pl.when(i == 6)
        def _():
            second_up.start()
            second_down.start()
            start_sides(*edges)

        @pl.when(i < 5)
        def _():
            start_sides(pair(i))

        @pl.when(i == 8)
        def _():
            await_sides(*edges)
            for copy in corners[0] + corners[1]:
                copy.start()

        @pl.when(conv == 1)
        def _():
            finish_second((low, high))

        @pl.when(i >= 8)
        def _():
            give(i - 8)

        return 0

    lax.fori_loop(0, 12, step, 0)

    def drain_in(q, _):
        for k in ORDER:
            in_copy(q, k).wait_send()
        return 0

    lax.fori_loop(0, QI, drain_in, 0)
    for copy in [field_up, field_down, second_up, second_down] + corners[0] + corners[1]:
        copy.wait_send()
    for s in [pair(p) for p in range(5)] + list(edges):
        for n in range(2):
            side(*s, n).wait_send()

    def drain_out(q, _):
        for k in ORDER:
            out_arrival(q, k).wait_recv()
            out_copy(q, k).wait_send()
        own_copy(q).wait()
        return 0

    lax.fori_loop(0, QO, drain_out, 0)


def assemble(parts, lat, out, wide, line):
    q = pl.program_id(0)
    for j in range(N):
        wide[j] = parts[j, 0].astype(F32)
    for r in range(RO):
        for j in range(N):
            line[r, j * W : (j + 1) * W] = wide[j, r * W : (r + 1) * W]
        at = (q * RO + r + OUT_FROM) % H
        out[at] = (line[r] + lat[at].astype(F32)).astype(BF16)


def on_device(lat, g1, w1, b1, g2, w2, b2):
    lat = lat.reshape(H, COLS, C)
    vmem, hbm = pl.BlockSpec(memory_space=pltpu.VMEM), pl.BlockSpec(memory_space=pl.ANY)
    dma = pltpu.SemaphoreType.DMA
    parts = pl.pallas_call(
        kernel,
        out_shape=jax.ShapeDtypeStruct((N, QO, PO, C), BF16),
        in_specs=[hbm, vmem, hbm, vmem, vmem, hbm, vmem],
        out_specs=hbm,
        scratch_shapes=[
            pltpu.VMEM((2, 9 * C, 3 * C), BF16),
            pltpu.VMEM((2, H + 2, WH, N, C), BF16),
            pltpu.VMEM((QI, N, PI, C), BF16),
            pltpu.VMEM((QI, N, PI, C), BF16),
            pltpu.VMEM((H, COLS, C), BF16),
            pltpu.VMEM((H, COLS + 16, C), F32),
            pltpu.VMEM((4, PI, C), F32),
            pltpu.VMEM((LANES, N * PI, 128), F32),
            pltpu.VMEM((2 * W * N, 3 * C), F32),
            pltpu.VMEM((LANES, N * QO * PO, 128), F32),
            pltpu.VMEM((QO, N, PO, C), BF16),
            dma((2, 3)), dma,
            dma((QI, N)), dma((QI, N)),
            dma((2,)), dma((2,)),
            dma((7, 2)), dma((7, 2)),
            dma((2,)), dma((2,)),
            dma((2, 2)), dma((2, 2)),
            dma((QO, N)), dma((QO, N)),
            dma((QO,)),
        ],
        compiler_params=pltpu.CompilerParams(
            collective_id=0, has_side_effects=True, vmem_limit_bytes=60 << 20
        ),
        name="block",
    )(lat, g1, w1, b1, g2, w2, b2)
    result = pl.pallas_call(
        assemble,
        out_shape=jax.ShapeDtypeStruct((H, COLS, C), BF16),
        grid=(QO,),
        in_specs=[
            pl.BlockSpec((N, 1, PO, C), lambda q: (0, q, 0, 0)),
            pl.BlockSpec((H, COLS, C), lambda q: (0, 0, 0)),
        ],
        out_specs=pl.BlockSpec((H, COLS, C), lambda q: (0, 0, 0)),
        scratch_shapes=[pltpu.VMEM((N, PO, C), F32), pltpu.VMEM((RO, COLS, C), F32)],
        compiler_params=pltpu.CompilerParams(vmem_limit_bytes=32 << 20),
        name="assemble",
    )(parts, lat)
    return result.reshape(1, H, COLS, C)


def solution(mesh):
    return jax.shard_map(
        on_device,
        mesh=mesh,
        in_specs=(P("tm", "rows", None, None), P(), P(), P(), P(), P(), P()),
        out_specs=P("tm", "rows", None, None),
        check_vma=False,
    )
```

```python
import functools

import jax
import jax.numpy as jnp
from jax import lax
from jax.experimental import pallas as pl
from jax.experimental.pallas import tpu as pltpu
from jax.sharding import PartitionSpec as P

MESH = pl.DeviceIdType.MESH
F32, BF16 = jnp.float32, jnp.bfloat16

C = 384
LANES = C // 128
H = 12
COLS = 160
N = 16
W = COLS // N
WH = W + 2
QI, RI = 3, 4
QO, RO = 4, 3
OUT_FROM = 2
PI = RI * WH
PO = 32


def norm_act(v, gain):
    scale = lax.rsqrt(jnp.mean(v * v, axis=-1, keepdims=True) + 1e-06)
    u = v * scale * gain
    half = 0.5 * u
    return half + half * jnp.tanh(half)


def later(v, frames):
    at = lax.broadcasted_iota(jnp.int32, v.shape, v.ndim - 2)
    return jnp.where(at < frames, 0.0, pltpu.roll(v, frames, v.ndim - 2))


def peer(me, k):
    z, x, c = me // 8, (me // 2) % 4, me % 2
    dz, dx, dc = k // 8, (k // 2) % 4, k % 2
    return ((z + dz) % 2) * 8 + ((x + dx) % 4) * 2 + (c + dc) % 2


def source(me, k):
    z, x, c = me // 8, (me // 2) % 4, me % 2
    dz, dx, dc = k // 8, (k // 2) % 4, k % 2
    return ((z + dz) % 2) * 8 + ((x + 4 - dx) % 4) * 2 + (c + dc) % 2


ORDER = (12, 13, 4, 5, 10, 11, 14, 15, 2, 3, 6, 7, 8, 9, 1)


def kernel(
    lat_hbm, g1, w1, b1, g2, w2, b2,
    out,
    wc, act, recv, send, lat, nrm, pk, tr, prod, otr, ostage,
    w_sem, lat_sem, in_send, in_recv, f_send, f_recv, c_send, c_recv, r_send, r_recv, k_send, k_recv,
    out_send, out_recv, own_sem,
):
    field, second = act.at[0], act.at[1]
    me = lax.axis_index("tm")
    row = lax.axis_index("rows")
    left, right = (me + N - 1) % N, (me + 1) % N
    up, down = (row + 7) % 8, (row + 1) % 8
    to = {k: peer(me, k) for k in ORDER}
    source_of = {k: source(me, k) for k in ORDER}

    barrier = pltpu.get_barrier_semaphore()
    for dev in (up, down):
        pl.semaphore_signal(barrier, inc=1, device_id=(me, dev), device_id_type=MESH)
    for k in ORDER:
        pl.semaphore_signal(barrier, inc=1, device_id=(to[k], row), device_id_type=MESH)

    lat_copy = pltpu.make_async_copy(lat_hbm, lat, lat_sem)
    lat_copy.start()

    def weight(i, a):
        return pltpu.make_async_copy(
            (w1, w2)[i].at[pl.ds(a * 9 * C, 9 * C)],
            wc.at[i, :, pl.ds((2 - a) * C, C)],
            w_sem.at[i, a],
        )

    for i in range(2):
        for a in range(3):
            weight(i, a).start()

    nrm[:, 0:8] = jnp.zeros((H, 8, C), F32)
    nrm[:, 8 + COLS : 16 + COLS] = jnp.zeros((H, 8, C), F32)
    otr[...] = jnp.zeros_like(otr)

    def in_copy(q, k):
        return pltpu.make_async_remote_copy(
            src_ref=send.at[q, to[k]],
            dst_ref=recv.at[q, me],
            send_sem=in_send.at[q, k],
            recv_sem=in_recv.at[q, k],
            device_id=(to[k], row),
            device_id_type=MESH,
        )

    def in_arrival(q, k):
        return pltpu.make_async_remote_copy(
            src_ref=send.at[q, to[k]],
            dst_ref=recv.at[q, source_of[k]],
            send_sem=in_send.at[q, k],
            recv_sem=in_recv.at[q, k],
            device_id=(to[k], row),
            device_id_type=MESH,
        )

    def norm_row(r, _):
        nrm[r, 8 : 8 + COLS] = norm_act(lat[r].astype(F32), g1[...].reshape(1, C))
        return 0

    def pack(q, _):
        for j in range(N):
            for n in range(RI):
                pk[j % 4, n * WH : (n + 1) * WH] = nrm[q * RI + n, j * W + 7 : j * W + 7 + WH]
            send[q, j] = pk[j % 4].astype(BF16)
        recv[q, me] = send[q, me]
        return 0

    def dispatch(q, _):
        for k in ORDER:
            in_copy(q, k).start()
        return 0

    lat_copy.wait()
    def ready(q, _):
        lax.fori_loop(q * RI, (q + 1) * RI, norm_row, 0)
        return pack(q, 0)

    ready(0, 0)
    pl.semaphore_wait(barrier, N - 1 + 2)
    dispatch(0, 0)

    def follow(q, _):
        ready(q, 0)
        return dispatch(q, 0)

    lax.fori_loop(1, QI, follow, 0)

    def row_halo(i, ref, at, target, dev, columns, s_sem, r_sem):
        return pltpu.make_async_remote_copy(
            src_ref=ref.at[at, columns], dst_ref=ref.at[target, columns],
            send_sem=s_sem.at[i], recv_sem=r_sem.at[i],
            device_id=(me, dev), device_id_type=MESH,
        )

    every, own = pl.ds(0, WH), pl.ds(1, W)
    field_up = row_halo(0, field, 1, H + 1, up, every, f_send, f_recv)
    field_down = row_halo(1, field, H, 0, down, every, f_send, f_recv)

    def arrive(q):
        for k in ORDER:
            in_arrival(q, k).wait_recv()

        def widen(f, _):
            v = recv[q, f].astype(F32)
            for lane in range(LANES):
                tr[lane, pl.ds(f * PI, PI)] = v[:, lane * 128 : (lane + 1) * 128]
            return 0

        lax.fori_loop(0, N, widen, 0, unroll=4)
        for n in (3, 0, 1, 2):

            def turn(c, _):
                v = [tr[lane, pl.ds(n * WH + c, N, stride=PI)] for lane in range(LANES)]
                field[1 + q * RI + n, c] = jnp.concatenate(v, axis=-1).astype(BF16)
                return 0

            lax.fori_loop(0, WH, turn, 0, unroll=True)
            if n == 3:

                @pl.when(q == QI - 1)
                def _():
                    field_down.start()
                    field_up.start()


    def multiply(conv, rows):
        taps = [
            jnp.concatenate([act[conv, r + b, e : e + W] for r in rows], axis=0).reshape(-1, C)
            for b in range(3) for e in range(3)
        ]
        prod[...] = jnp.dot(
            jnp.concatenate(taps, axis=-1), wc[conv], preferred_element_type=F32
        )

    def collect(px, count):
        v = prod[pl.ds(px * N, count * N)].reshape(count, N, 3 * C)
        return v[:, :, :C] + later(v[:, :, C : 2 * C], 1) + later(v[:, :, 2 * C :], 2)

    def side(i, at, rows, which):
        src, dst, dev = ((1, W + 1, left), (W, 0, right))[which]
        return pltpu.make_async_remote_copy(
            src_ref=second.at[pl.ds(at, rows), pl.ds(src, 1)],
            dst_ref=second.at[pl.ds(at, rows), pl.ds(dst, 1)],
            send_sem=c_send.at[i, which], recv_sem=c_recv.at[i, which],
            device_id=(dev, row), device_id_type=MESH,
        )

    edges = ((5, 1, 1), (6, H, 1))

    def pair(p):
        return (p, 2 * p + 2, 2)

    def start_sides(*which):
        for s in which:
            for n in range(2):
                side(*s, n).start()

    def await_sides(*which):
        for s in which:
            for n in range(2):
                side(*s, n).wait_recv()
            _, at, rows = s

            @pl.when(me == 0)
            def _():
                second[pl.ds(at, rows), 0] = jnp.zeros((rows, N, C), BF16)

            @pl.when(me == N - 1)
            def _():
                second[pl.ds(at, rows), W + 1] = jnp.zeros((rows, N, C), BF16)

    corners = []
    for i, (at, target, dev) in enumerate(((1, H + 1, up), (H, 0, down))):
        corners.append([
            row_halo(n, second, at, target, dev, pl.ds(column, 1), k_send.at[i], k_recv.at[i])
            for n, column in enumerate((0, W + 1))
        ])

    second_up = row_halo(0, second, 1, H + 1, up, own, r_send, r_recv)
    second_down = row_halo(1, second, H, 0, down, own, r_send, r_recv)

    def out_copy(q, k):
        return pltpu.make_async_remote_copy(
            src_ref=ostage.at[q, to[k]],
            dst_ref=out.at[me, q],
            send_sem=out_send.at[q, k],
            recv_sem=out_recv.at[q, k],
            device_id=(to[k], row),
            device_id_type=MESH,
        )

    def out_arrival(q, k):
        return pltpu.make_async_remote_copy(
            src_ref=ostage.at[q, to[k]],
            dst_ref=out.at[source_of[k], q],
            send_sem=out_send.at[q, k],
            recv_sem=out_recv.at[q, k],
            device_id=(to[k], row),
            device_id_type=MESH,
        )

    def own_copy(q):
        return pltpu.make_async_copy(ostage.at[q, me], out.at[me, q], own_sem.at[q])

    def finish_first(rows):
        for n, r in enumerate(rows):

            def some(g, _):
                v = collect(n * W + g * 2, 2) + b1[...].reshape(1, C)
                v = norm_act(v, g2[...].reshape(1, C))
                second[r + 1, pl.ds(1 + g * 2, 2)] = v.astype(BF16)
                return 0

            lax.fori_loop(0, W // 2, some, 0, unroll=True)

    def finish_second(rows):
        for n, r in enumerate(rows):

            def some(c, _):
                v = collect(n * W + c, 1)[0] + b2[...].reshape(1, C)
                slot = (r + H - OUT_FROM) % H
                px = (slot // RO) * PO + (slot % RO) * W + c
                for lane in range(LANES):
                    otr[lane, pl.ds(px, N, stride=QO * PO)] = v[:, lane * 128 : (lane + 1) * 128]
                return 0

            lax.fori_loop(0, W, some, 0, unroll=True)

    def give(q):
        def narrow(f, _):
            v = [otr[lane, pl.ds((f * QO + q) * PO, PO)] for lane in range(LANES)]
            ostage[q, f] = jnp.concatenate(v, axis=-1).astype(BF16)
            return 0

        lax.fori_loop(0, N, narrow, 0, unroll=4)
        for k in ORDER:
            out_copy(q, k).start()
        own_copy(q).start()

    def clear(ref, at, missing):
        @pl.when(row == missing)
        def _():
            ref[at] = jnp.zeros((WH, N, C), BF16)

    def table(i, values):
        value = values[0]
        for n in range(1, len(values)):
            value = jnp.where(i == n, values[n], value)
        return value

    def step(i, _):
        conv = table(i, (0, 0, 0, 0, 0, 1, 0, 1, 1, 1, 1, 1))
        low = table(i, (1, 3, 5, 7, 9, 2, 0, 4, 6, 8, 1, 0))
        high = table(i, (2, 4, 6, 8, 10, 3, 11, 5, 7, 9, 10, 11))

        @pl.when((i == 0) | (i == 1) | (i == 3))
        def _():
            arrive(i - i // 3)

        @pl.when(i == 0)
        def _():
            for a in range(3):
                weight(0, a).wait()

        @pl.when(i == 5)
        def _():
            for a in range(3):
                weight(1, a).wait()
            await_sides(pair(0), pair(1))

        @pl.when(i == 6)
        def _():
            field_down.wait_recv()
            clear(field, 0, 0)
            field_up.wait_recv()
            clear(field, H + 1, 7)

        @pl.when((i >= 7) & (i <= 9))
        def _():
            await_sides(pair(i - 5))

        @pl.when(i == 11)
        def _():
            for copy in [second_down, second_up] + corners[0] + corners[1]:
                copy.wait_recv()
            clear(second, 0, 0)
            clear(second, H + 1, 7)

        multiply(conv, (low, high))

        @pl.when(conv == 0)
        def _():
            finish_first((low, high))

        @pl.when(i == 6)
        def _():
            second_up.start()
            second_down.start()
            start_sides(*edges)

        @pl.when(i < 5)
        def _():
            start_sides(pair(i))

        @pl.when(i == 7)
        def _():
            await_sides(*edges)
            for copy in corners[0] + corners[1]:
                copy.start()

        @pl.when(conv == 1)
        def _():
            finish_second((low, high))

        @pl.when(i >= 8)
        def _():
            give(i - 8)

        return 0

    lax.fori_loop(0, 12, step, 0)

    def drain_in(q, _):
        for k in ORDER:
            in_copy(q, k).wait_send()
        return 0

    lax.fori_loop(0, QI, drain_in, 0)
    for copy in [field_up, field_down, second_up, second_down] + corners[0] + corners[1]:
        copy.wait_send()
    for s in [pair(p) for p in range(5)] + list(edges):
        for n in range(2):
            side(*s, n).wait_send()

    def drain_out(q, _):
        for k in ORDER:
            out_arrival(q, k).wait_recv()
            out_copy(q, k).wait_send()
        own_copy(q).wait()
        return 0

    lax.fori_loop(0, QO, drain_out, 0)


def assemble(parts, lat, out, wide, line):
    q = pl.program_id(0)
    for j in range(N):
        wide[j] = parts[j, 0].astype(F32)
    for r in range(RO):
        for j in range(N):
            line[r, j * W : (j + 1) * W] = wide[j, r * W : (r + 1) * W]
        at = (q * RO + r + OUT_FROM) % H
        out[at] = (line[r] + lat[at].astype(F32)).astype(BF16)


def on_device(lat, g1, w1, b1, g2, w2, b2):
    lat = lat.reshape(H, COLS, C)
    vmem, hbm = pl.BlockSpec(memory_space=pltpu.VMEM), pl.BlockSpec(memory_space=pl.ANY)
    dma = pltpu.SemaphoreType.DMA
    parts = pl.pallas_call(
        kernel,
        out_shape=jax.ShapeDtypeStruct((N, QO, PO, C), BF16),
        in_specs=[hbm, vmem, hbm, vmem, vmem, hbm, vmem],
        out_specs=hbm,
        scratch_shapes=[
            pltpu.VMEM((2, 9 * C, 3 * C), BF16),
            pltpu.VMEM((2, H + 2, WH, N, C), BF16),
            pltpu.VMEM((QI, N, PI, C), BF16),
            pltpu.VMEM((QI, N, PI, C), BF16),
            pltpu.VMEM((H, COLS, C), BF16),
            pltpu.VMEM((H, COLS + 16, C), F32),
            pltpu.VMEM((4, PI, C), F32),
            pltpu.VMEM((LANES, N * PI, 128), F32),
            pltpu.VMEM((2 * W * N, 3 * C), F32),
            pltpu.VMEM((LANES, N * QO * PO, 128), F32),
            pltpu.VMEM((QO, N, PO, C), BF16),
            dma((2, 3)), dma,
            dma((QI, N)), dma((QI, N)),
            dma((2,)), dma((2,)),
            dma((7, 2)), dma((7, 2)),
            dma((2,)), dma((2,)),
            dma((2, 2)), dma((2, 2)),
            dma((QO, N)), dma((QO, N)),
            dma((QO,)),
        ],
        compiler_params=pltpu.CompilerParams(
            collective_id=0, has_side_effects=True, vmem_limit_bytes=60 << 20
        ),
        name="block",
    )(lat, g1, w1, b1, g2, w2, b2)
    result = pl.pallas_call(
        assemble,
        out_shape=jax.ShapeDtypeStruct((H, COLS, C), BF16),
        grid=(QO,),
        in_specs=[
            pl.BlockSpec((N, 1, PO, C), lambda q: (0, q, 0, 0)),
            pl.BlockSpec((H, COLS, C), lambda q: (0, 0, 0)),
        ],
        out_specs=pl.BlockSpec((H, COLS, C), lambda q: (0, 0, 0)),
        scratch_shapes=[pltpu.VMEM((N, PO, C), F32), pltpu.VMEM((RO, COLS, C), F32)],
        compiler_params=pltpu.CompilerParams(vmem_limit_bytes=32 << 20),
        name="assemble",
    )(parts, lat)
    return result.reshape(1, H, COLS, C)


def solution(mesh):
    return jax.shard_map(
        on_device,
        mesh=mesh,
        in_specs=(P("tm", "rows", None, None), P(), P(), P(), P(), P(), P()),
        out_specs=P("tm", "rows", None, None),
        check_vma=False,
    )
```
